32 devices in a mesh: row: 4 (over y, x), col: 8 (over z, core).
Axes of the slice: x: 2, y: 2, z: 4, core: 2. Of those that a mesh axis runs over, the one named last changes fastest.
Arguments:
- tokens: bfloat16 [128, 256, 1024], P(('row', 'col')), may hold values from -7 to 7
- phi: bfloat16 [1024, 32], replicated, may hold values from -5 to 5
- w_in: bfloat16 [32, 1024, 2048], P(('row', 'col')), may hold values from -0.1875 to 0.1875
- w_out: bfloat16 [32, 2048, 1024], P(('row', 'col')), may hold values from -0.125 to 0.125
- cotangent: bfloat16 [128, 256, 1024], P(('row', 'col')), may hold values from -6 to 6
Outputs:
- mixed: bfloat16 [128, 256, 1024], P(('row', 'col'))
- grad_tokens: bfloat16 [128, 256, 1024], P(('row', 'col'))
- grad_phi: float32 [1024, 32], P(None, ('row', 'col'))
- grad_w_in: bfloat16 [32, 1024, 2048], P(('row', 'col'))
- grad_w_out: bfloat16 [32, 2048, 1024], P(('row', 'col'))
The draws below stay inside these ranges and needn't reach their ends.
All inputs are finite; a program needn't handle non-finite values.
Results may differ from the reference program's by a relative error of at most 0.015.
Values may be sent and summed in bfloat16 or wider, within the bound.
A program may use at most 128 MiB of HBM per device.

```python
import math
import jax
import jax.numpy as jnp
from jax import lax

D = 1024
HID = 2048
PATCHES = 256
IMG_DEV = 4
EXPERTS = 32
IMAGES = 128


def drawn_rows(key):
    return jnp.clip(jax.random.normal(jax.random.fold_in(key, 101), (4, D), jnp.float32), -4.5, 4.5)


def drawn_strengths():
    return jnp.array([150.0, 300.0, 450.0, 600.0], jnp.float32)


def draw_tokens(key, part):
    total = IMG_DEV * EXPERTS
    values = jnp.clip(jax.random.normal(jax.random.fold_in(key, 11), (total, PATCHES, D), jnp.float32), -4.5, 4.5)
    planted = drawn_rows(key)
    noise = jnp.clip(jax.random.normal(jax.random.fold_in(key, 12), (4, D), jnp.float32), -4.5, 4.5)
    nearby = planted * (1.0 - 2.0 / drawn_strengths())[:, None] + 0.1 * noise
    places = jnp.arange(4) * (total // 4)
    values = values.at[places, 0].set(planted)
    values = values.at[places, 1].set(nearby)
    return values.astype(jnp.bfloat16)


def draw_phi(key, part):
    values = jnp.clip(jax.random.normal(jax.random.fold_in(key, 21), (D, EXPERTS), jnp.float32), -4.5, 4.5) * D ** (-0.5)
    return values.astype(jnp.bfloat16)


def block_levels(rng, extent, split, low, top_value):
    def one(axis_at, parts):
        draws = jax.random.uniform(jax.random.fold_in(jax.random.fold_in(rng, 6), axis_at), (parts,), jnp.float32, low / len(split), top_value / len(split))
        return jnp.repeat(jnp.exp(draws), extent[axis_at] // parts).reshape((-1,) + (1,) * (len(extent) - axis_at - 1))

    gain = one(*split[0])
    for cut in split[1:]:
        gain = gain * one(*cut)
    return gain


def normal_values(rng, extent, spread, most, shards=(), held_as=jnp.bfloat16):
    values = jax.random.normal(rng, extent, jnp.float32) * spread
    if len(shards) > 0:
        values = block_levels(rng, extent, shards, -0.22, 0.18) * values
    return jnp.clip(values, min=-most, max=most).astype(held_as)


def setup_inputs(seed: int = 0) -> dict:
    seeds = jax.random.split(jax.random.key(seed), 6)
    tokens = draw_tokens(jax.random.fold_in(seeds[5], 71), 0)
    phi = draw_phi(jax.random.fold_in(seeds[5], 71), 0)
    w_in = normal_values(seeds[2], (EXPERTS, D, HID), D ** -0.5, 0.1875, ((0, 32),))
    w_out = normal_values(seeds[3], (EXPERTS, HID, D), HID ** -0.5, 0.125, ((0, 32),))
    cotangent = normal_values(seeds[4], (IMAGES, PATCHES, D), 1.0, 6.0, ((0, 32),))
    return {"tokens": tokens, "phi": phi, "w_in": w_in, "w_out": w_out, "cotangent": cotangent}


def gelu_parts(pre_act):
    const = math.sqrt(2.0 / math.pi)
    inner = const * (pre_act + 0.044715 * pre_act ** 3)
    tanh_val = jnp.tanh(inner)
    value = 0.5 * pre_act * (1.0 + tanh_val)
    slope = 0.5 * (1.0 + tanh_val) + 0.5 * pre_act * (1.0 - tanh_val * tanh_val) * const * (1.0 + 3.0 * 0.044715 * pre_act * pre_act)
    return (value, slope)

def forward_one(inputs):
    expert_rows, weight_a, weight_b = inputs
    pre_act = jnp.dot(expert_rows, weight_a, preferred_element_type=jnp.float32)
    hidden = gelu_parts(pre_act)[0].astype(jnp.bfloat16)
    return jnp.dot(hidden, weight_b, preferred_element_type=jnp.float32).astype(jnp.bfloat16)

def backward_one(inputs):
    expert_rows, grad_rows, weight_a, weight_b = inputs
    pre_act = jnp.dot(expert_rows, weight_a, preferred_element_type=jnp.float32)
    value, slope = gelu_parts(pre_act)
    hidden = value.astype(jnp.bfloat16)
    grad_b = jnp.dot(hidden.T, grad_rows, preferred_element_type=jnp.float32).astype(jnp.bfloat16)
    d_hidden = jnp.dot(grad_rows, weight_b.T, preferred_element_type=jnp.float32)
    d_pre = (d_hidden * slope).astype(jnp.bfloat16)
    grad_a = jnp.dot(expert_rows.T, d_pre, preferred_element_type=jnp.float32).astype(jnp.bfloat16)
    d_rows = jnp.dot(d_pre, weight_a.T, preferred_element_type=jnp.float32).astype(jnp.bfloat16)
    return (grad_a, grad_b, d_rows)

def reference(tokens, phi, w_in, w_out, cotangent):
    f32 = jnp.float32
    token_vals = tokens.astype(f32)
    phi_vals = phi.astype(f32)
    logits = jnp.einsum('bmd,ds->bms', token_vals, phi_vals)
    dispatch = jax.nn.softmax(logits, axis=1)
    combine = jax.nn.softmax(logits, axis=2)
    dispatch_b = dispatch.astype(jnp.bfloat16)
    combine_b = combine.astype(jnp.bfloat16)
    slot_in = jnp.einsum('bms,bmd->bsd', dispatch_b.astype(f32), token_vals).astype(jnp.bfloat16)
    slot_out = lax.map(forward_one, (jnp.swapaxes(slot_in, 0, 1), w_in, w_out))
    slot_out = jnp.swapaxes(slot_out, 0, 1)
    mixed = jnp.einsum('bms,bsd->bmd', combine_b.astype(f32), slot_out.astype(f32)).astype(jnp.bfloat16)
    grad_vals = cotangent.astype(f32)
    d_slot_out = jnp.einsum('bms,bmd->bsd', combine_b.astype(f32), grad_vals).astype(jnp.bfloat16)
    d_combine = jnp.einsum('bmd,bsd->bms', grad_vals, slot_out.astype(f32))
    d_logits_c = combine * (d_combine - lax.optimization_barrier(jnp.sum(combine * d_combine, axis=2, keepdims=True)))
    grad_w_in, grad_w_out, d_rows = lax.map(backward_one, (jnp.swapaxes(slot_in, 0, 1), jnp.swapaxes(d_slot_out, 0, 1), w_in, w_out))
    d_slot_in = jnp.swapaxes(d_rows, 0, 1)
    d_dispatch = jnp.einsum('bmd,bsd->bms', token_vals, d_slot_in.astype(f32))
    d_logits = (d_logits_c + dispatch * (d_dispatch - lax.optimization_barrier(jnp.sum(dispatch * d_dispatch, axis=1, keepdims=True)))).astype(jnp.bfloat16)
    grad_tokens = (jnp.einsum('bms,bsd->bmd', dispatch_b.astype(f32), d_slot_in.astype(f32)) + jnp.einsum('bms,ds->bmd', d_logits.astype(f32), phi_vals)).astype(jnp.bfloat16)
    grad_phi = jnp.einsum('bmd,bms->ds', token_vals, d_logits.astype(f32))
    return (mixed, grad_tokens, grad_phi, grad_w_in, grad_w_out)
```

```python
import math

import jax
import jax.numpy as jnp
from jax import lax
from jax.sharding import PartitionSpec as P


def gelu_parts(pre_act):
    const = math.sqrt(2.0 / math.pi)
    inner = const * (pre_act + 0.044715 * pre_act**3)
    tanh_val = jnp.tanh(inner)
    value = 0.5 * pre_act * (1.0 + tanh_val)
    slope = 0.5 * (1.0 + tanh_val) + 0.5 * pre_act * (1.0 - tanh_val * tanh_val) * const * (
        1.0 + 3.0 * 0.044715 * pre_act * pre_act
    )
    return (value, slope)


def send_slots(slots):
    return lax.all_to_all(slots, ("row", "col"), split_axis=1, concat_axis=1, tiled=True)


def return_results(slots):
    return lax.all_to_all(slots, ("row", "col"), split_axis=1, concat_axis=1, tiled=True)


def send_out_grads(slots):
    return lax.all_to_all(slots, ("row", "col"), split_axis=1, concat_axis=1, tiled=True)


def return_in_grads(slots):
    return lax.all_to_all(slots, ("row", "col"), split_axis=1, concat_axis=1, tiled=True)


def on_device(tokens, phi, w_in, w_out, cotangent):
    f32 = jnp.float32
    images, patches, feature_dim = tokens.shape
    logits = jnp.einsum("imd,ds->ims", tokens, phi, preferred_element_type=f32)
    dispatch = jax.nn.softmax(logits, axis=1)
    combine = jax.nn.softmax(logits, axis=2)
    dispatch_b = dispatch.astype(jnp.bfloat16)
    combine_b = combine.astype(jnp.bfloat16)
    slot_in = jnp.einsum("ims,imd->isd", dispatch_b, tokens, preferred_element_type=f32).astype(
        jnp.bfloat16
    )
    expert_in = send_slots(slot_in)
    expert_rows = expert_in.reshape(-1, feature_dim)
    weight_a = w_in[0]
    weight_b = w_out[0]
    pre_act = jnp.dot(expert_rows, weight_a, preferred_element_type=f32)
    value, slope = gelu_parts(pre_act)
    hidden = value.astype(jnp.bfloat16)
    expert_out = jnp.dot(hidden, weight_b, preferred_element_type=f32).astype(jnp.bfloat16)
    slot_out = return_results(expert_out.reshape(expert_in.shape))
    mixed = jnp.einsum("ims,isd->imd", combine_b, slot_out, preferred_element_type=f32).astype(
        jnp.bfloat16
    )
    d_slot_out = jnp.einsum(
        "ims,imd->isd", combine_b, cotangent, preferred_element_type=f32
    ).astype(jnp.bfloat16)
    grad_rows = send_out_grads(d_slot_out).reshape(-1, feature_dim)
    d_combine = jnp.einsum("imd,isd->ims", cotangent, slot_out, preferred_element_type=f32)
    d_logits_c = combine * (d_combine - jnp.sum(combine * d_combine, axis=2, keepdims=True))
    grad_b = jnp.einsum("rh,rd->hd", hidden, grad_rows, preferred_element_type=f32).astype(
        jnp.bfloat16
    )
    d_hidden = jnp.einsum("rd,hd->rh", grad_rows, weight_b, preferred_element_type=f32)
    d_pre = (d_hidden * slope).astype(jnp.bfloat16)
    grad_a = jnp.einsum("rd,rh->dh", expert_rows, d_pre, preferred_element_type=f32).astype(
        jnp.bfloat16
    )
    d_rows = jnp.einsum("rh,dh->rd", d_pre, weight_a, preferred_element_type=f32).astype(
        jnp.bfloat16
    )
    d_slot_in = return_in_grads(d_rows.reshape(expert_in.shape))
    d_dispatch = jnp.einsum("imd,isd->ims", tokens, d_slot_in, preferred_element_type=f32)
    d_logits = (
        d_logits_c + dispatch * (d_dispatch - jnp.sum(dispatch * d_dispatch, axis=1, keepdims=True))
    ).astype(jnp.bfloat16)
    grad_tokens = (
        jnp.einsum("ims,isd->imd", dispatch_b, d_slot_in, preferred_element_type=f32)
        + jnp.einsum("ims,ds->imd", d_logits, phi, preferred_element_type=f32)
    ).astype(jnp.bfloat16)
    phi_terms = jnp.einsum("ims,imd->sd", d_logits, tokens, preferred_element_type=f32)
    shares = lax.all_to_all(phi_terms, ("row", "col"), split_axis=0, concat_axis=0, tiled=True)
    grad_phi = jnp.sum(shares, axis=0)[:, None]
    return (mixed, grad_tokens, grad_phi, grad_a[None], grad_b[None])


def solution(mesh):
    placed = (
        P(("row", "col"), None, None),
        P(),
        P(("row", "col"), None, None),
        P(("row", "col"), None, None),
        P(("row", "col"), None, None),
    )
    return jax.shard_map(
        on_device,
        mesh=mesh,
        in_specs=placed,
        out_specs=(
            P(("row", "col"), None, None),
            P(("row", "col"), None, None),
            P(None, ("row", "col")),
            P(("row", "col"), None, None),
            P(("row", "col"), None, None),
        ),
        check_vma=False,
    )
```

```python
import functools
import math

import jax
import jax.numpy as jnp
from jax import lax
from jax.experimental import pallas as pl
from jax.experimental.pallas import tpu as pltpu
from jax.sharding import PartitionSpec as P

F32 = jnp.float32
BF16 = jnp.bfloat16
MESH = pl.DeviceIdType.MESH
SLAB = 16


def gelu_parts(pre_act):
    const = math.sqrt(2.0 / math.pi)
    inner = const * (pre_act + 0.044715 * pre_act**3)
    tanh_val = jnp.tanh(inner)
    value = 0.5 * pre_act * (1.0 + tanh_val)
    slope = 0.5 * (1.0 + tanh_val) + 0.5 * pre_act * (1.0 - tanh_val * tanh_val) * const * (
        1.0 + 3.0 * 0.044715 * pre_act * pre_act
    )
    return (value, slope)


def dot(a, b, dims):
    return lax.dot_general(a, b, (dims, ((), ())), preferred_element_type=F32)


NN = ((1,), (0,))
NT = ((1,), (1,))
TN = ((0,), (0,))


def permutation(minor, group):
    size = minor * group
    shift = minor.bit_length() - 1
    row = lax.broadcasted_iota(jnp.int32, (size, size), 0)
    column = lax.broadcasted_iota(jnp.int32, (size, size), 1)
    source = (row & (minor - 1)) * group + (row >> shift)
    return jnp.where(column == source, 1.0, 0.0).astype(BF16)


def permutation_back(minor, group):
    size = minor * group
    shift = minor.bit_length() - 1
    row = lax.broadcasted_iota(jnp.int32, (size, size), 0)
    column = lax.broadcasted_iota(jnp.int32, (size, size), 1)
    source = (column & (minor - 1)) * group + (column >> shift)
    return jnp.where(row == source, 1.0, 0.0).astype(BF16)


def exchange_kernel(
    n, cols, images,
    tok_hbm, phi_t, w_in_hbm, w_out_hbm, cot_hbm,
    x_ref, hid_ref, dpre_ref, g_ref, so_ref, dsi_ref, disp_b, comb_b, dl_b, gphi_ref,
    tok, cot, w_in, w_out, rows, slope, disp, comb, perm, perm_back,
    sends, recvs, send_phi, recv_phi,
    load_sem, send_sem, recv_sem,
):
    patches, dim = tok.shape[0] // images, tok.shape[1]
    hid = w_in.shape[1]
    group = min(32, n)
    chunks = SLAB // images
    lanes = dim // chunks
    me = lax.axis_index("row") * cols + lax.axis_index("col")

    loads = [
        pltpu.make_async_copy(src, dst, load_sem.at[k])
        for k, (src, dst) in enumerate(
            ((tok_hbm, tok), (cot_hbm, cot), (w_in_hbm, w_in), (w_out_hbm, w_out))
        )
    ]
    for load in loads:
        load.start()

    barrier = pltpu.get_barrier_semaphore()

    def greet(j, carry):
        d = lax.rem(me + j, n)
        pl.semaphore_signal(barrier, inc=1, device_id=(d // cols, lax.rem(d, cols)), device_id_type=MESH)
        return carry

    lax.fori_loop(1, n, greet, 0)

    def start(k, src, dst):
        def one(j, carry):
            d = lax.rem(me + j, n)
            pltpu.make_async_remote_copy(
                src_ref=src.at[d], dst_ref=dst.at[me],
                send_sem=send_sem.at[k], recv_sem=recv_sem.at[k],
                device_id=(d // cols, lax.rem(d, cols)), device_id_type=MESH,
            ).start()
            return carry

        lax.fori_loop(1, n, one, 0)
        dst[me] = src[me]

    def whole(k, src, dst):
        d = lax.rem(me + 1, n)
        return pltpu.make_async_remote_copy(
            src_ref=src.at[pl.ds(0, n - 1)], dst_ref=dst.at[pl.ds(0, n - 1)],
            send_sem=send_sem.at[k], recv_sem=recv_sem.at[k],
            device_id=(d // cols, lax.rem(d, cols)), device_id_type=MESH,
        )

    def pack(src, dst):
        for g in range(n // group):
            parts = [
                src[i * n + g * group : i * n + (g + 1) * group, q * lanes : (q + 1) * lanes]
                for q in range(chunks)
                for i in range(images)
            ]
            out = dot(perm[...], jnp.concatenate(parts, axis=0), NN).astype(BF16)
            dst[g * group : (g + 1) * group] = out.reshape(group, SLAB, lanes)

    def unpack(src, dst):
        for g in range(n // group):
            slab = src[g * group : (g + 1) * group].reshape(group * SLAB, lanes)
            out = dot(perm_back[...], slab, NN).astype(BF16)
            for q in range(chunks):
                for i in range(images):
                    at = (q * images + i) * group
                    dst[i * n + g * group : i * n + (g + 1) * group, q * lanes : (q + 1) * lanes] = out[
                        at : at + group
                    ]

    perm[...] = permutation(SLAB, group)
    perm_back[...] = permutation_back(SLAB, group)

    loads[0].wait()
    for i in range(images):
        mine = tok[i * patches : (i + 1) * patches]
        logits = dot(phi_t[...], mine, NT)
        e = jnp.exp(logits - jnp.max(logits, axis=1, keepdims=True))
        dispatch = e / jnp.sum(e, axis=1, keepdims=True)
        disp[i] = dispatch
        disp_b[i] = dispatch.astype(BF16)
        e = jnp.exp(logits - jnp.max(logits, axis=0, keepdims=True))
        combine = e / jnp.sum(e, axis=0, keepdims=True)
        comb[i] = combine
        comb_b[i] = combine.astype(BF16)
        rows[i * n : (i + 1) * n] = dot(dispatch.astype(BF16), mine, NN).astype(BF16)
    pack(rows, sends.at[0])
    pl.semaphore_wait(barrier, n - 1)
    start(0, sends.at[0], recvs.at[0])

    loads[1].wait()
    for i in range(images):
        mine = cot[i * patches : (i + 1) * patches]
        rows[i * n : (i + 1) * n] = dot(comb_b[i], mine, NN).astype(BF16)
    pack(rows, sends.at[1])
    start(1, sends.at[1], recvs.at[1])

    loads[2].wait()
    loads[3].wait()
    wide = min(512, hid)
    thin = min(256, dim)

    whole(0, sends.at[0], recvs.at[0]).wait_recv()
    unpack(recvs.at[0], x_ref)

    @pl.loop(0, hid // wide)
    def _(c):
        at = pl.ds(pl.multiple_of(c * wide, wide), wide)
        value, grad = gelu_parts(dot(x_ref[...], w_in[:, at], NN))
        hid_ref[:, at] = value.astype(BF16)
        slope[:, at] = grad

    @pl.loop(0, dim // thin)
    def _(c):
        at = pl.ds(pl.multiple_of(c * thin, thin), thin)
        rows[:, at] = dot(hid_ref[...], w_out[:, at], NN).astype(BF16)

    pack(rows, sends.at[2])
    start(2, sends.at[2], recvs.at[2])

    whole(1, sends.at[1], recvs.at[1]).wait_recv()
    unpack(recvs.at[1], g_ref)

    @pl.loop(0, hid // wide)
    def _(c):
        at = pl.ds(pl.multiple_of(c * wide, wide), wide)
        dpre_ref[:, at] = (dot(g_ref[...], w_out[at, :], NT) * slope[:, at]).astype(BF16)

    @pl.loop(0, dim // thin)
    def _(c):
        at = pl.ds(pl.multiple_of(c * thin, thin), thin)
        rows[:, at] = dot(dpre_ref[...], w_in[at, :], NT).astype(BF16)

    pack(rows, sends.at[3])
    start(3, sends.at[3], recvs.at[3])

    whole(2, sends.at[2], recvs.at[2]).wait_recv()
    unpack(recvs.at[2], so_ref)
    for i in range(images):
        d_combine = dot(so_ref[i * n : (i + 1) * n], cot[i * patches : (i + 1) * patches], NT)
        combine = comb[i]
        comb[i] = combine * (d_combine - jnp.sum(combine * d_combine, axis=0, keepdims=True))

    whole(3, sends.at[3], recvs.at[3]).wait_recv()
    unpack(recvs.at[3], dsi_ref)
    terms = jnp.zeros((n, dim), F32)
    for i in range(images):
        mine = tok[i * patches : (i + 1) * patches]
        d_dispatch = dot(dsi_ref[i * n : (i + 1) * n], mine, NT)
        dispatch = disp[i]
        d_logits = comb[i] + dispatch * (
            d_dispatch - jnp.sum(dispatch * d_dispatch, axis=1, keepdims=True)
        )
        d_logits = d_logits.astype(BF16)
        dl_b[i] = d_logits
        terms = terms + dot(d_logits, mine, NN)

    minor = dim // 128
    phi_perm = permutation(minor, group)
    for g in range(n // group):
        some = terms[g * group : (g + 1) * group]
        flat = jnp.concatenate([some[:, j * 128 : (j + 1) * 128] for j in range(minor)], axis=0)
        high = flat.astype(BF16)
        rest = flat - high.astype(F32)
        middle = rest.astype(BF16)
        low = (rest - middle.astype(F32)).astype(BF16)
        out = dot(phi_perm, jnp.concatenate([high, middle, low], axis=1), NN)
        out = (out[:, :128] + out[:, 128:256]) + out[:, 256:]
        send_phi[g * group : (g + 1) * group] = out.reshape(group, minor, 128)
    start(4, send_phi, recv_phi)
    whole(4, send_phi, recv_phi).wait_recv()
    gphi_ref[...] = jnp.sum(recv_phi[...], axis=0)

    for k in range(4):
        whole(k, sends.at[k], recvs.at[k]).wait_send()
    whole(4, send_phi, recv_phi).wait_send()


def outputs_kernel(
    x_ref, dpre_ref, hid_ref, g_ref, comb_b, so_ref, disp_b, dl_b, dsi_ref, phi_t,
    mixed_ref, gtok_ref, gin_ref, gout_ref,
):
    gin_ref[0] = dot(x_ref[...], dpre_ref[...], TN).astype(BF16)
    gout_ref[0] = dot(hid_ref[...], g_ref[...], TN).astype(BF16)
    mixed_ref[0] = dot(comb_b[0], so_ref[...], TN).astype(BF16)
    left = jnp.concatenate([disp_b[0], dl_b[0]], axis=0)
    right = jnp.concatenate([dsi_ref[...], phi_t[...]], axis=0)
    gtok_ref[0] = dot(left, right, TN).astype(BF16)


def on_device(n, cols, tokens, phi, w_in, w_out, cotangent):
    images, patches, dim = tokens.shape
    hid = w_in.shape[2]
    count = images * n
    group = min(32, n)
    lanes = dim * images // SLAB
    minor = dim // 128
    phi_t = phi.T
    any_ = pl.BlockSpec(memory_space=pl.ANY)
    vmem = pl.BlockSpec(memory_space=pltpu.VMEM)

    def shape(*s, t=BF16):
        return jax.ShapeDtypeStruct(s, t)

    x, hidden, d_pre, grads, so, dsi, disp_b, comb_b, dl_b, gphi = pl.pallas_call(
        functools.partial(exchange_kernel, n, cols, images),
        out_shape=(
            shape(count, dim), shape(count, hid), shape(count, hid), shape(count, dim),
            shape(count, dim), shape(count, dim),
            shape(images, n, patches), shape(images, n, patches), shape(images, n, patches),
            shape(minor, 128, t=F32),
        ),
        in_specs=[any_, vmem, any_, any_, any_],
        out_specs=(vmem,) * 10,
        scratch_shapes=[
            pltpu.VMEM((images * patches, dim), BF16),
            pltpu.VMEM((images * patches, dim), BF16),
            pltpu.VMEM((dim, hid), BF16),
            pltpu.VMEM((hid, dim), BF16),
            pltpu.VMEM((count, dim), BF16),
            pltpu.VMEM((count, hid), F32),
            pltpu.VMEM((images, n, patches), F32),
            pltpu.VMEM((images, n, patches), F32),
            pltpu.VMEM((SLAB * group, SLAB * group), BF16),
            pltpu.VMEM((SLAB * group, SLAB * group), BF16),
            pltpu.VMEM((4, n, SLAB, lanes), BF16),
            pltpu.VMEM((4, n, SLAB, lanes), BF16),
            pltpu.VMEM((n, minor, 128), F32),
            pltpu.VMEM((n, minor, 128), F32),
            pltpu.SemaphoreType.DMA((4,)),
            pltpu.SemaphoreType.DMA((5,)),
            pltpu.SemaphoreType.DMA((5,)),
        ],
        compiler_params=pltpu.CompilerParams(
            collective_id=0, has_side_effects=True, vmem_limit_bytes=56 * 1024 * 1024
        ),
        name="exchange",
    )(
        tokens.reshape(images * patches, dim), phi_t, w_in[0], w_out[0],
        cotangent.reshape(images * patches, dim),
    )

    steps = 2 * images
    half = patches // 2
    turned = pl.BlockSpec((1, n, half), lambda j: (j // 2, 0, j % 2))
    image = pl.BlockSpec((n, dim), lambda j: (j // 2, 0))

    def fixed(*s):
        return pl.BlockSpec(s, lambda j: (0,) * len(s))

    mixed, grad_tokens, grad_a, grad_b = pl.pallas_call(
        outputs_kernel,
        grid=(steps,),
        out_shape=(
            shape(images, patches, dim), shape(images, patches, dim),
            shape(1, dim, hid), shape(1, hid, dim),
        ),
        in_specs=[
            pl.BlockSpec((count, dim // steps), lambda j: (0, j)),
            fixed(count, hid),
            pl.BlockSpec((count, hid // steps), lambda j: (0, j)),
            fixed(count, dim),
            turned, image, turned, turned, image,
            fixed(n, dim),
        ],
        out_specs=(
            pl.BlockSpec((1, half, dim), lambda j: (j // 2, j % 2, 0)),
            pl.BlockSpec((1, half, dim), lambda j: (j // 2, j % 2, 0)),
            pl.BlockSpec((1, dim // steps, hid), lambda j: (0, j, 0)),
            pl.BlockSpec((1, hid // steps, dim), lambda j: (0, j, 0)),
        ),
        compiler_params=pltpu.CompilerParams(vmem_limit_bytes=48 * 1024 * 1024),
        name="outputs",
    )(x, d_pre, hidden, grads, comb_b, so, disp_b, dl_b, dsi, phi_t)
    return (mixed, grad_tokens, gphi.reshape(dim, 1), grad_a, grad_b)


def solution(mesh):
    cols = mesh.shape["col"]
    n = mesh.shape["row"] * cols
    split = P(("row", "col"), None, None)
    return jax.shard_map(
        functools.partial(on_device, n, cols),
        mesh=mesh,
        in_specs=(split, P(), split, split, split),
        out_specs=(split, split, P(None, ("row", "col")), split, split),
        check_vma=False,
    )
```

```python
import functools
import math

import jax
import jax.numpy as jnp
from jax import lax
from jax.experimental import pallas as pl
from jax.experimental.pallas import tpu as pltpu
from jax.sharding import PartitionSpec as P

F32 = jnp.float32
BF16 = jnp.bfloat16
MESH = pl.DeviceIdType.MESH
SLAB = 16


def gelu_parts(pre_act):
    const = math.sqrt(2.0 / math.pi)
    inner = const * (pre_act + 0.044715 * pre_act**3)
    tanh_val = jnp.tanh(inner)
    value = 0.5 * pre_act * (1.0 + tanh_val)
    slope = 0.5 * (1.0 + tanh_val) + 0.5 * pre_act * (1.0 - tanh_val * tanh_val) * const * (
        1.0 + 3.0 * 0.044715 * pre_act * pre_act
    )
    return (value, slope)


def dot(a, b, dims):
    return lax.dot_general(a, b, (dims, ((), ())), preferred_element_type=F32)


NN = ((1,), (0,))
NT = ((1,), (1,))
TN = ((0,), (0,))


def permutation(minor, group):
    size = minor * group
    shift = minor.bit_length() - 1
    row = lax.broadcasted_iota(jnp.int32, (size, size), 0)
    column = lax.broadcasted_iota(jnp.int32, (size, size), 1)
    source = (row & (minor - 1)) * group + (row >> shift)
    return jnp.where(column == source, 1.0, 0.0).astype(BF16)


def permutation_back(minor, group):
    size = minor * group
    shift = minor.bit_length() - 1
    row = lax.broadcasted_iota(jnp.int32, (size, size), 0)
    column = lax.broadcasted_iota(jnp.int32, (size, size), 1)
    source = (column & (minor - 1)) * group + (column >> shift)
    return jnp.where(row == source, 1.0, 0.0).astype(BF16)


def exchange_kernel(
    n, cols, images,
    tok_hbm, phi_t, w_in_hbm, w_out_hbm, cot_hbm,
    x_ref, hid_ref, dpre_ref, g_ref, so_ref, dsi_ref, disp_b, comb_b, dl_b, gphi_ref,
    tok, cot, w_in, w_out, rows, slope, disp, comb, perm, perm_back,
    sends, recvs, send_phi, recv_phi,
    load_sem, send_sem, recv_sem,
):
    patches, dim = tok.shape[0] // images, tok.shape[1]
    hid = w_in.shape[1]
    group = min(32, n)
    chunks = SLAB // images
    lanes = dim // chunks
    me = lax.axis_index("row") * cols + lax.axis_index("col")

    loads = [
        pltpu.make_async_copy(src, dst, load_sem.at[k])
        for k, (src, dst) in enumerate(
            ((tok_hbm, tok), (cot_hbm, cot), (w_in_hbm, w_in), (w_out_hbm, w_out))
        )
    ]
    loads[0].start()
    loads[1].start()

    barrier = pltpu.get_barrier_semaphore()

    def greet(j, carry):
        d = lax.rem(me + j, n)
        pl.semaphore_signal(barrier, inc=1, device_id=(d // cols, lax.rem(d, cols)), device_id_type=MESH)
        return carry

    lax.fori_loop(1, n, greet, 0)

    def start(k, src, dst):
        def one(j, carry):
            d = lax.rem(me + j, n)
            pltpu.make_async_remote_copy(
                src_ref=src.at[d], dst_ref=dst.at[me],
                send_sem=send_sem.at[k], recv_sem=recv_sem.at[k],
                device_id=(d // cols, lax.rem(d, cols)), device_id_type=MESH,
            ).start()
            return carry

        lax.fori_loop(1, n, one, 0)
        dst[me] = src[me]

    def whole(k, src, dst):
        d = lax.rem(me + 1, n)
        return pltpu.make_async_remote_copy(
            src_ref=src.at[pl.ds(0, n - 1)], dst_ref=dst.at[pl.ds(0, n - 1)],
            send_sem=send_sem.at[k], recv_sem=recv_sem.at[k],
            device_id=(d // cols, lax.rem(d, cols)), device_id_type=MESH,
        )

    def pack(src, dst):
        for g in range(n // group):
            parts = [
                src[i * n + g * group : i * n + (g + 1) * group, q * lanes : (q + 1) * lanes]
                for q in range(chunks)
                for i in range(images)
            ]
            out = dot(perm[...], jnp.concatenate(parts, axis=0), NN).astype(BF16)
            dst[g * group : (g + 1) * group] = out.reshape(group, SLAB, lanes)

    def unpack(src, dst):
        for g in range(n // group):
            slab = src[g * group : (g + 1) * group].reshape(group * SLAB, lanes)
            out = dot(perm_back[...], slab, NN).astype(BF16)
            for q in range(chunks):
                for i in range(images):
                    at = (q * images + i) * group
                    dst[i * n + g * group : i * n + (g + 1) * group, q * lanes : (q + 1) * lanes] = out[
                        at : at + group
                    ]

    perm[...] = permutation(SLAB, group)

    loads[0].wait()
    loads[2].start()
    loads[3].start()
    for i in range(images):
        mine = tok[i * patches : (i + 1) * patches]
        logits = dot(phi_t[...], mine, NT)
        e = jnp.exp(logits - jnp.max(logits, axis=1, keepdims=True))
        dispatch = e / jnp.sum(e, axis=1, keepdims=True)
        disp[i] = dispatch
        disp_b[i] = dispatch.astype(BF16)
        e = jnp.exp(logits - jnp.max(logits, axis=0, keepdims=True))
        combine = e / jnp.sum(e, axis=0, keepdims=True)
        comb[i] = combine
        comb_b[i] = combine.astype(BF16)
        rows[i * n : (i + 1) * n] = dot(dispatch.astype(BF16), mine, NN).astype(BF16)
    pack(rows, sends.at[0])
    pl.semaphore_wait(barrier, n - 1)
    start(0, sends.at[0], recvs.at[0])

    loads[1].wait()
    for i in range(images):
        mine = cot[i * patches : (i + 1) * patches]
        rows[i * n : (i + 1) * n] = dot(comb_b[i], mine, NN).astype(BF16)
    pack(rows, sends.at[1])
    start(1, sends.at[1], recvs.at[1])
    perm_back[...] = permutation_back(SLAB, group)

    loads[2].wait()
    loads[3].wait()
    wide = min(512, hid)
    thin = min(256, dim)

    whole(0, sends.at[0], recvs.at[0]).wait_recv()
    unpack(recvs.at[0], x_ref)

    @pl.loop(0, hid // wide)
    def _(c):
        at = pl.ds(pl.multiple_of(c * wide, wide), wide)
        value, grad = gelu_parts(dot(x_ref[...], w_in[:, at], NN))
        hid_ref[:, at] = value.astype(BF16)
        slope[:, at] = grad

    @pl.loop(0, dim // thin)
    def _(c):
        at = pl.ds(pl.multiple_of(c * thin, thin), thin)
        rows[:, at] = dot(hid_ref[...], w_out[:, at], NN).astype(BF16)

    pack(rows, sends.at[2])
    start(2, sends.at[2], recvs.at[2])

    whole(1, sends.at[1], recvs.at[1]).wait_recv()
    unpack(recvs.at[1], g_ref)

    @pl.loop(0, hid // wide)
    def _(c):
        at = pl.ds(pl.multiple_of(c * wide, wide), wide)
        dpre_ref[:, at] = (dot(g_ref[...], w_out[at, :], NT) * slope[:, at]).astype(BF16)

    @pl.loop(0, dim // thin)
    def _(c):
        at = pl.ds(pl.multiple_of(c * thin, thin), thin)
        rows[:, at] = dot(dpre_ref[...], w_in[at, :], NT).astype(BF16)

    pack(rows, sends.at[3])
    start(3, sends.at[3], recvs.at[3])

    whole(2, sends.at[2], recvs.at[2]).wait_recv()
    unpack(recvs.at[2], so_ref)
    for i in range(images):
        d_combine = dot(so_ref[i * n : (i + 1) * n], cot[i * patches : (i + 1) * patches], NT)
        combine = comb[i]
        comb[i] = combine * (d_combine - jnp.sum(combine * d_combine, axis=0, keepdims=True))

    whole(3, sends.at[3], recvs.at[3]).wait_recv()
    unpack(recvs.at[3], dsi_ref)
    terms = jnp.zeros((n, dim), F32)
    for i in range(images):
        mine = tok[i * patches : (i + 1) * patches]
        d_dispatch = dot(dsi_ref[i * n : (i + 1) * n], mine, NT)
        dispatch = disp[i]
        d_logits = comb[i] + dispatch * (
            d_dispatch - jnp.sum(dispatch * d_dispatch, axis=1, keepdims=True)
        )
        d_logits = d_logits.astype(BF16)
        dl_b[i] = d_logits
        terms = terms + dot(d_logits, mine, NN)

    minor = dim // 128
    phi_perm = permutation(minor, group)
    for g in range(n // group):
        some = terms[g * group : (g + 1) * group]
        flat = jnp.concatenate([some[:, j * 128 : (j + 1) * 128] for j in range(minor)], axis=0)
        high = flat.astype(BF16)
        rest = flat - high.astype(F32)
        middle = rest.astype(BF16)
        low = (rest - middle.astype(F32)).astype(BF16)
        out = dot(phi_perm, jnp.concatenate([high, middle, low], axis=1), NN)
        out = (out[:, :128] + out[:, 128:256]) + out[:, 256:]
        send_phi[g * group : (g + 1) * group] = out.reshape(group, minor, 128)
    start(4, send_phi, recv_phi)
    whole(4, send_phi, recv_phi).wait_recv()
    gphi_ref[...] = jnp.sum(recv_phi[...], axis=0)

    for k in range(4):
        whole(k, sends.at[k], recvs.at[k]).wait_send()
    whole(4, send_phi, recv_phi).wait_send()


def outputs_kernel(
    images,
    x_ref, dpre_ref, hid_ref, g_ref, comb_b, so_ref, disp_b, dl_b, dsi_ref, phi_t, gphi_ref,
    mixed_hbm, gtok_hbm, gin_hbm, gout_hbm, column_ref,
    mixed, gtok, gin, gout, sem,
):
    n = phi_t.shape[0]
    copies = []

    def put(k, j, src, dst, size):
        at = pl.ds(j * size, size)
        copy = pltpu.make_async_copy(src.at[at], dst.at[at], sem.at[k, j])
        copy.start()
        copies.append(copy)

    wide = gin.shape[0] // images
    tall = gout.shape[0] // images
    for j in range(images):
        at = slice(j * wide, (j + 1) * wide)
        gin[at] = dot(x_ref[:, at], dpre_ref[...], TN).astype(BF16)
        put(0, j, gin, gin_hbm.at[0], wide)
        at = slice(j * tall, (j + 1) * tall)
        gout[at] = dot(hid_ref[:, at], g_ref[...], TN).astype(BF16)
        put(1, j, gout, gout_hbm.at[0], tall)
        at = slice(j * n, (j + 1) * n)
        mixed[j] = dot(comb_b[j], so_ref[at], TN).astype(BF16)
        put(2, j, mixed, mixed_hbm, 1)
        left = jnp.concatenate([disp_b[j], dl_b[j]], axis=0)
        right = jnp.concatenate([dsi_ref[at], phi_t[...]], axis=0)
        gtok[j] = dot(left, right, TN).astype(BF16)
        put(3, j, gtok, gtok_hbm, 1)
    for j in range(gphi_ref.shape[0]):
        column_ref[:, j * 128 : (j + 1) * 128] = gphi_ref[j : j + 1, :]
    for copy in copies:
        copy.wait()


def on_device(n, cols, tokens, phi, w_in, w_out, cotangent):
    images, patches, dim = tokens.shape
    hid = w_in.shape[2]
    count = images * n
    group = min(32, n)
    lanes = dim * images // SLAB
    minor = dim // 128
    phi_t = phi.T
    any_ = pl.BlockSpec(memory_space=pl.ANY)
    vmem = pl.BlockSpec(memory_space=pltpu.VMEM)

    def shape(*s, t=BF16):
        return jax.ShapeDtypeStruct(s, t)

    x, hidden, d_pre, grads, so, dsi, disp_b, comb_b, dl_b, gphi = pl.pallas_call(
        functools.partial(exchange_kernel, n, cols, images),
        out_shape=(
            shape(count, dim), shape(count, hid), shape(count, hid), shape(count, dim),
            shape(count, dim), shape(count, dim),
            shape(images, n, patches), shape(images, n, patches), shape(images, n, patches),
            shape(minor, 128, t=F32),
        ),
        in_specs=[any_, vmem, any_, any_, any_],
        out_specs=(vmem,) * 10,
        scratch_shapes=[
            pltpu.VMEM((images * patches, dim), BF16),
            pltpu.VMEM((images * patches, dim), BF16),
            pltpu.VMEM((dim, hid), BF16),
            pltpu.VMEM((hid, dim), BF16),
            pltpu.VMEM((count, dim), BF16),
            pltpu.VMEM((count, hid), F32),
            pltpu.VMEM((images, n, patches), F32),
            pltpu.VMEM((images, n, patches), F32),
            pltpu.VMEM((SLAB * group, SLAB * group), BF16),
            pltpu.VMEM((SLAB * group, SLAB * group), BF16),
            pltpu.VMEM((4, n, SLAB, lanes), BF16),
            pltpu.VMEM((4, n, SLAB, lanes), BF16),
            pltpu.VMEM((n, minor, 128), F32),
            pltpu.VMEM((n, minor, 128), F32),
            pltpu.SemaphoreType.DMA((4,)),
            pltpu.SemaphoreType.DMA((5,)),
            pltpu.SemaphoreType.DMA((5,)),
        ],
        compiler_params=pltpu.CompilerParams(
            collective_id=0, has_side_effects=True, vmem_limit_bytes=56 * 1024 * 1024
        ),
        name="exchange",
    )(
        tokens.reshape(images * patches, dim), phi_t, w_in[0], w_out[0],
        cotangent.reshape(images * patches, dim),
    )

    mixed, grad_tokens, grad_a, grad_b, grad_phi = pl.pallas_call(
        functools.partial(outputs_kernel, images),
        out_shape=(
            shape(images, patches, dim), shape(images, patches, dim),
            shape(1, dim, hid), shape(1, hid, dim), shape(1, dim, t=F32),
        ),
        in_specs=[vmem] * 11,
        out_specs=(any_,) * 4 + (vmem,),
        scratch_shapes=[
            pltpu.VMEM((images, patches, dim), BF16),
            pltpu.VMEM((images, patches, dim), BF16),
            pltpu.VMEM((dim, hid), BF16),
            pltpu.VMEM((hid, dim), BF16),
            pltpu.SemaphoreType.DMA((4, images)),
        ],
        compiler_params=pltpu.CompilerParams(vmem_limit_bytes=63 * 1024 * 1024 + 768 * 1024),
        name="outputs",
    )(x, d_pre, hidden, grads, comb_b, so, disp_b, dl_b, dsi, phi_t, gphi)
    return (mixed, grad_tokens, grad_phi.reshape(dim, 1), grad_a, grad_b)


def solution(mesh):
    cols = mesh.shape["col"]
    n = mesh.shape["row"] * cols
    split = P(("row", "col"), None, None)
    return jax.shard_map(
        functools.partial(on_device, n, cols),
        mesh=mesh,
        in_specs=(split, P(), split, split, split),
        out_specs=(split, split, P(None, ("row", "col")), split, split),
        check_vma=False,
    )
```

```python
import functools
import math

import jax
import jax.numpy as jnp
from jax import lax
from jax.experimental import pallas as pl
from jax.experimental.pallas import tpu as pltpu
from jax.sharding import PartitionSpec as P

F32 = jnp.float32
BF16 = jnp.bfloat16
MESH = pl.DeviceIdType.MESH
SLAB = 16


def gelu_parts(pre_act):
    const = math.sqrt(2.0 / math.pi)
    inner = const * (pre_act + 0.044715 * pre_act**3)
    tanh_val = jnp.tanh(inner)
    value = 0.5 * pre_act * (1.0 + tanh_val)
    slope = 0.5 * (1.0 + tanh_val) + 0.5 * pre_act * (1.0 - tanh_val * tanh_val) * const * (
        1.0 + 3.0 * 0.044715 * pre_act * pre_act
    )
    return (value, slope)


def dot(a, b, dims):
    return lax.dot_general(a, b, (dims, ((), ())), preferred_element_type=F32)


NN = ((1,), (0,))
NT = ((1,), (1,))
TN = ((0,), (0,))


def permutation(minor, group):
    size = minor * group
    shift = minor.bit_length() - 1
    row = lax.broadcasted_iota(jnp.int32, (size, size), 0)
    column = lax.broadcasted_iota(jnp.int32, (size, size), 1)
    source = (row & (minor - 1)) * group + (row >> shift)
    return jnp.where(column == source, 1.0, 0.0).astype(BF16)


def permutation_back(minor, group):
    size = minor * group
    shift = minor.bit_length() - 1
    row = lax.broadcasted_iota(jnp.int32, (size, size), 0)
    column = lax.broadcasted_iota(jnp.int32, (size, size), 1)
    source = (column & (minor - 1)) * group + (column >> shift)
    return jnp.where(row == source, 1.0, 0.0).astype(BF16)


def exchange_kernel(
    n, cols, images,
    tok_hbm, phi_t, w_in_hbm, w_out_hbm, cot_hbm,
    x_ref, hid_ref, dpre_ref, g_ref, so_ref, dsi_ref, disp_b, comb_b, dl_b, gphi_ref,
    tok, cot, w_in, w_out, rows, slope, disp, comb, perm, perm_back,
    sends, recvs, send_phi, recv_phi,
    load_sem, send_sem, recv_sem,
):
    patches, dim = tok.shape[0] // images, tok.shape[1]
    hid = w_in.shape[1]
    group = min(32, n)
    chunks = SLAB // images
    lanes = dim // chunks
    me = lax.axis_index("row") * cols + lax.axis_index("col")

    loads = [
        pltpu.make_async_copy(src, dst, load_sem.at[k])
        for k, (src, dst) in enumerate(
            ((tok_hbm, tok), (cot_hbm, cot), (w_in_hbm, w_in), (w_out_hbm, w_out))
        )
    ]
    loads[0].start()
    loads[1].start()

    barrier = pltpu.get_barrier_semaphore()

    def greet(j, carry):
        d = lax.rem(me + j, n)
        pl.semaphore_signal(barrier, inc=1, device_id=(d // cols, lax.rem(d, cols)), device_id_type=MESH)
        return carry

    lax.fori_loop(1, n, greet, 0, unroll=n <= 32)

    def start(k, src, dst):
        stride = 13 if math.gcd(13, n) == 1 else 1

        def one(j, carry):
            d = lax.rem(me + j * stride, n)
            pltpu.make_async_remote_copy(
                src_ref=src.at[d], dst_ref=dst.at[me],
                send_sem=send_sem.at[k], recv_sem=recv_sem.at[k],
                device_id=(d // cols, lax.rem(d, cols)), device_id_type=MESH,
            ).start()
            return carry

        lax.fori_loop(1, n, one, 0, unroll=n <= 32)
        dst[me] = src[me]

    def whole(k, src, dst):
        d = lax.rem(me + 1, n)
        return pltpu.make_async_remote_copy(
            src_ref=src.at[pl.ds(0, n - 1)], dst_ref=dst.at[pl.ds(0, n - 1)],
            send_sem=send_sem.at[k], recv_sem=recv_sem.at[k],
            device_id=(d // cols, lax.rem(d, cols)), device_id_type=MESH,
        )

    def pack(src, dst):
        for g in range(n // group):
            parts = [
                src[i * n + g * group : i * n + (g + 1) * group, q * lanes : (q + 1) * lanes]
                for q in range(chunks)
                for i in range(images)
            ]
            out = dot(perm[...], jnp.concatenate(parts, axis=0), NN).astype(BF16)
            dst[g * group : (g + 1) * group] = out.reshape(group, SLAB, lanes)

    def unpack(src, dst):
        for g in range(n // group):
            slab = src[g * group : (g + 1) * group].reshape(group * SLAB, lanes)
            out = dot(perm_back[...], slab, NN).astype(BF16)
            for q in range(chunks):
                for i in range(images):
                    at = (q * images + i) * group
                    dst[i * n + g * group : i * n + (g + 1) * group, q * lanes : (q + 1) * lanes] = out[
                        at : at + group
                    ]

    perm[...] = permutation(SLAB, group)

    loads[0].wait()
    loads[2].start()
    loads[3].start()
    for i in range(images):
        mine = tok[i * patches : (i + 1) * patches]
        logits = dot(phi_t[...], mine, NT)
        e = jnp.exp(logits - jnp.max(logits, axis=1, keepdims=True))
        dispatch = e / jnp.sum(e, axis=1, keepdims=True)
        disp[i] = dispatch
        disp_b[i] = dispatch.astype(BF16)
        e = jnp.exp(logits - jnp.max(logits, axis=0, keepdims=True))
        combine = e / jnp.sum(e, axis=0, keepdims=True)
        comb[i] = combine
        comb_b[i] = combine.astype(BF16)
        rows[i * n : (i + 1) * n] = dot(dispatch.astype(BF16), mine, NN).astype(BF16)
    pack(rows, sends.at[0])
    pl.semaphore_wait(barrier, n - 1)
    start(0, sends.at[0], recvs.at[0])

    loads[1].wait()
    for i in range(images):
        mine = cot[i * patches : (i + 1) * patches]
        rows[i * n : (i + 1) * n] = dot(comb_b[i], mine, NN).astype(BF16)
    pack(rows, sends.at[1])
    start(1, sends.at[1], recvs.at[1])
    perm_back[...] = permutation_back(SLAB, group)

    loads[2].wait()
    loads[3].wait()
    wide = min(512, hid)
    thin = min(256, dim)

    whole(0, sends.at[0], recvs.at[0]).wait_recv()
    unpack(recvs.at[0], x_ref)

    @pl.loop(0, hid // wide)
    def _(c):
        at = pl.ds(pl.multiple_of(c * wide, wide), wide)
        pre_act = dot(x_ref[...], w_in[:, at], NN)
        hid_ref[:, at] = gelu_parts(pre_act)[0].astype(BF16)
        slope[:, at] = pre_act

    @pl.loop(0, dim // thin)
    def _(c):
        at = pl.ds(pl.multiple_of(c * thin, thin), thin)
        rows[:, at] = dot(hid_ref[...], w_out[:, at], NN).astype(BF16)

    pack(rows, sends.at[2])
    start(2, sends.at[2], recvs.at[2])

    @pl.loop(0, hid // wide)
    def _(c):
        at = pl.ds(pl.multiple_of(c * wide, wide), wide)
        slope[:, at] = gelu_parts(slope[:, at])[1]

    whole(1, sends.at[1], recvs.at[1]).wait_recv()
    unpack(recvs.at[1], g_ref)

    @pl.loop(0, hid // wide)
    def _(c):
        at = pl.ds(pl.multiple_of(c * wide, wide), wide)
        dpre_ref[:, at] = (dot(g_ref[...], w_out[at, :], NT) * slope[:, at]).astype(BF16)

    @pl.loop(0, dim // thin)
    def _(c):
        at = pl.ds(pl.multiple_of(c * thin, thin), thin)
        rows[:, at] = dot(dpre_ref[...], w_in[at, :], NT).astype(BF16)

    pack(rows, sends.at[3])
    start(3, sends.at[3], recvs.at[3])

    whole(2, sends.at[2], recvs.at[2]).wait_recv()
    unpack(recvs.at[2], so_ref)
    for i in range(images):
        d_combine = dot(so_ref[i * n : (i + 1) * n], cot[i * patches : (i + 1) * patches], NT)
        combine = comb[i]
        comb[i] = combine * (d_combine - jnp.sum(combine * d_combine, axis=0, keepdims=True))

    whole(3, sends.at[3], recvs.at[3]).wait_recv()
    unpack(recvs.at[3], dsi_ref)
    terms = jnp.zeros((n, dim), F32)
    for i in range(images):
        mine = tok[i * patches : (i + 1) * patches]
        d_dispatch = dot(dsi_ref[i * n : (i + 1) * n], mine, NT)
        dispatch = disp[i]
        d_logits = comb[i] + dispatch * (
            d_dispatch - jnp.sum(dispatch * d_dispatch, axis=1, keepdims=True)
        )
        d_logits = d_logits.astype(BF16)
        dl_b[i] = d_logits
        terms = terms + dot(d_logits, mine, NN)

    minor = dim // 128
    phi_perm = permutation(minor, group)
    for g in range(n // group):
        some = terms[g * group : (g + 1) * group]
        flat = jnp.concatenate([some[:, j * 128 : (j + 1) * 128] for j in range(minor)], axis=0)
        high = flat.astype(BF16)
        rest = flat - high.astype(F32)
        middle = rest.astype(BF16)
        low = (rest - middle.astype(F32)).astype(BF16)
        out = dot(phi_perm, jnp.concatenate([high, middle, low], axis=1), NN)
        out = (out[:, :128] + out[:, 128:256]) + out[:, 256:]
        send_phi[g * group : (g + 1) * group] = out.reshape(group, minor, 128)
    start(4, send_phi, recv_phi)
    whole(4, send_phi, recv_phi).wait_recv()
    gphi_ref[...] = jnp.sum(recv_phi[...], axis=0)

    for k in range(4):
        whole(k, sends.at[k], recvs.at[k]).wait_send()
    whole(4, send_phi, recv_phi).wait_send()


def outputs_kernel(
    images,
    x_ref, dpre_ref, hid_ref, g_ref, comb_b, so_ref, disp_b, dl_b, dsi_ref, phi_t, gphi_ref,
    mixed_hbm, gtok_hbm, gin_hbm, gout_hbm, column_ref,
    mixed, gtok, gin, gout, sem,
):
    n = phi_t.shape[0]
    copies = []

    def put(k, j, src, dst, size):
        at = pl.ds(j * size, size)
        copy = pltpu.make_async_copy(src.at[at], dst.at[at], sem.at[k, j])
        copy.start()
        copies.append(copy)

    wide = gin.shape[0] // images
    tall = gout.shape[0] // images
    for j in range(images):
        at = slice(j * wide, (j + 1) * wide)
        gin[at] = dot(x_ref[:, at], dpre_ref[...], TN).astype(BF16)
        put(0, j, gin, gin_hbm.at[0], wide)
        at = slice(j * tall, (j + 1) * tall)
        gout[at] = dot(hid_ref[:, at], g_ref[...], TN).astype(BF16)
        put(1, j, gout, gout_hbm.at[0], tall)
        at = slice(j * n, (j + 1) * n)
        mixed[j] = dot(comb_b[j], so_ref[at], TN).astype(BF16)
        put(2, j, mixed, mixed_hbm, 1)
        left = jnp.concatenate([disp_b[j], dl_b[j]], axis=0)
        right = jnp.concatenate([dsi_ref[at], phi_t[...]], axis=0)
        gtok[j] = dot(left, right, TN).astype(BF16)
        put(3, j, gtok, gtok_hbm, 1)
    for j in range(gphi_ref.shape[0]):
        column_ref[:, j * 128 : (j + 1) * 128] = gphi_ref[j : j + 1, :]
    for copy in copies:
        copy.wait()


def on_device(n, cols, tokens, phi, w_in, w_out, cotangent):
    images, patches, dim = tokens.shape
    hid = w_in.shape[2]
    count = images * n
    group = min(32, n)
    lanes = dim * images // SLAB
    minor = dim // 128
    phi_t = phi.T
    any_ = pl.BlockSpec(memory_space=pl.ANY)
    vmem = pl.BlockSpec(memory_space=pltpu.VMEM)

    def shape(*s, t=BF16):
        return jax.ShapeDtypeStruct(s, t)

    x, hidden, d_pre, grads, so, dsi, disp_b, comb_b, dl_b, gphi = pl.pallas_call(
        functools.partial(exchange_kernel, n, cols, images),
        out_shape=(
            shape(count, dim), shape(count, hid), shape(count, hid), shape(count, dim),
            shape(count, dim), shape(count, dim),
            shape(images, n, patches), shape(images, n, patches), shape(images, n, patches),
            shape(minor, 128, t=F32),
        ),
        in_specs=[any_, vmem, any_, any_, any_],
        out_specs=(vmem,) * 10,
        scratch_shapes=[
            pltpu.VMEM((images * patches, dim), BF16),
            pltpu.VMEM((images * patches, dim), BF16),
            pltpu.VMEM((dim, hid), BF16),
            pltpu.VMEM((hid, dim), BF16),
            pltpu.VMEM((count, dim), BF16),
            pltpu.VMEM((count, hid), F32),
            pltpu.VMEM((images, n, patches), F32),
            pltpu.VMEM((images, n, patches), F32),
            pltpu.VMEM((SLAB * group, SLAB * group), BF16),
            pltpu.VMEM((SLAB * group, SLAB * group), BF16),
            pltpu.VMEM((4, n, SLAB, lanes), BF16),
            pltpu.VMEM((4, n, SLAB, lanes), BF16),
            pltpu.VMEM((n, minor, 128), F32),
            pltpu.VMEM((n, minor, 128), F32),
            pltpu.SemaphoreType.DMA((4,)),
            pltpu.SemaphoreType.DMA((5,)),
            pltpu.SemaphoreType.DMA((5,)),
        ],
        compiler_params=pltpu.CompilerParams(
            collective_id=0, has_side_effects=True, vmem_limit_bytes=56 * 1024 * 1024
        ),
        name="exchange",
    )(
        tokens.reshape(images * patches, dim), phi_t, w_in[0], w_out[0],
        cotangent.reshape(images * patches, dim),
    )

    mixed, grad_tokens, grad_a, grad_b, grad_phi = pl.pallas_call(
        functools.partial(outputs_kernel, images),
        out_shape=(
            shape(images, patches, dim), shape(images, patches, dim),
            shape(1, dim, hid), shape(1, hid, dim), shape(1, dim, t=F32),
        ),
        in_specs=[vmem] * 11,
        out_specs=(any_,) * 4 + (vmem,),
        scratch_shapes=[
            pltpu.VMEM((images, patches, dim), BF16),
            pltpu.VMEM((images, patches, dim), BF16),
            pltpu.VMEM((dim, hid), BF16),
            pltpu.VMEM((hid, dim), BF16),
            pltpu.SemaphoreType.DMA((4, images)),
        ],
        compiler_params=pltpu.CompilerParams(vmem_limit_bytes=63 * 1024 * 1024 + 768 * 1024),
        name="outputs",
    )(x, d_pre, hidden, grads, comb_b, so, disp_b, dl_b, dsi, phi_t, gphi)
    return (mixed, grad_tokens, grad_phi.reshape(dim, 1), grad_a, grad_b)


def solution(mesh):
    cols = mesh.shape["col"]
    n = mesh.shape["row"] * cols
    split = P(("row", "col"), None, None)
    return jax.shard_map(
        functools.partial(on_device, n, cols),
        mesh=mesh,
        in_specs=(split, P(), split, split, split),
        out_specs=(split, split, P(None, ("row", "col")), split, split),
        check_vma=False,
    )
```
